32 devices in a mesh: groups: 2 (over y), expert: 4 (over z), attn: 2 (over x), tp: 2 (over core).
Axes of the slice: x: 2, y: 2, z: 4, core: 2. Of those that a mesh axis runs over, the one named last changes fastest.
Arguments:
- queries: bfloat16 [16, 64, 128], P(('groups', 'expert', 'attn'), 'tp'), parts along dimension 0, may hold values from -8 to 8
- new_keys: bfloat16 [16, 4, 128], P(('groups', 'expert', 'attn'), 'tp'), parts along dimension 0, may hold values from -6 to 6
- new_values: bfloat16 [16, 4, 128], P(('groups', 'expert', 'attn'), 'tp'), parts along dimension 0, may hold values from -6 to 6
- kv_cache: bfloat16 [64, 64, 2, 4, 128], P(('groups', 'expert', 'attn'), None, None, 'tp'), parts along dimension 0, may hold values from -8 to 8
- block_tables: int32 [16, 4], P(('groups', 'expert', 'attn')), parts along dimension 0, may hold values from 0 to 3, as said below
- cache_lengths: int32 [16], P(('groups', 'expert', 'attn')), parts along dimension 0, may hold values from 3 to 256, as said below
- tokens: bfloat16 [1024, 2048], P(('groups', 'expert', 'attn', 'tp')), parts along dimension 0, may hold values from -200 to 200
- gain: float32 [2048], replicated, may hold values from 0.5 to 1.5
- expert_ids: int32 [1024, 8], P(('groups', 'expert', 'attn', 'tp')), parts along dimension 0, may hold values from 0 to 15, all different within a row; in each aligned block of 32 rows (0 to 31, 32 to 63, ...) at most 17 rows name the same one
- gate_weights: float32 [1024, 8], P(('groups', 'expert', 'attn', 'tp')), parts along dimension 0, may hold values from 0.05 to 1
- w_in: bfloat16 [16, 2, 1536, 2048], P(('expert', 'attn', 'tp')), may hold values from -0.125 to 0.125
- w_out: bfloat16 [16, 1536, 2048], P(('expert', 'attn', 'tp')), may hold values from -0.15625 to 0.15625
Outputs:
- attn_out: bfloat16 [16, 64, 128], P(('groups', 'expert', 'attn'), 'tp'), parts along dimension 0
- moe_out: bfloat16 [1024, 2048], P(('groups', 'expert', 'attn', 'tp')), parts along dimension 0
The draws below stay inside these ranges and needn't reach their ends.
There are 2 independent parts, one for each index of `groups`. The reference program is written for one: setup_inputs(seed, part) draws one part's arguments, and reference() takes and returns one part's arrays. A program takes and returns all parts, laid end to end along the dimension named above; an argument that names none is the same for every part. Nothing has to cross between parts.
Inputs may be any that keep to these rules, and one draw needn't show every extreme that they name: `block_tables`: within each attention group of 1 rows the entries are the page numbers of that group, each once. `cache_lengths`: some row holds exactly 256 cached tokens. `expert_ids`: each row names 8 different experts; within each aligned block of 32 rows (the rows of one device) no expert is named more than 17 times, and in some block some expert exactly 17 times; every expert is named somewhere.
All inputs are finite; a program needn't handle non-finite values.
Results may differ from the reference program's by a relative error of at most 0.0071.
Values may be sent and summed in bfloat16 or wider, within the bound.
A program may use at most 64 MiB of HBM per device.

```python
import math
from functools import partial
import jax
import jax.numpy as jnp
import numpy as np
from jax import lax

D = 2048
FF = 1536
HQ = 64
KVH = 4
HD = 128
TOP = 8
PAGE = 64
MAXBLK = 4
AR_DEV = 1
MROWS_DEV = 32
EXPERTS = 16
SLICES = 1
UNITS = 1536
MOST = 17
MROWS = 512
AROWS = 8
POOL = 4
POOLS = 32
MAXLEN = 256


def draw_queries(key, part):
    key = jax.random.fold_in(key, 11)
    base_key = jax.random.fold_in(key, 0)
    shape = (AROWS, HQ, HD)
    values = jnp.clip(jax.random.normal(base_key, shape, jnp.float32), -6.0, 6.0)
    return values.astype(jnp.bfloat16)


def draw_kv_cache(key, part):
    key = jax.random.fold_in(key, 12)
    shape = (POOLS, PAGE, 2, KVH, HD)
    values = jnp.clip(jax.random.normal(key, shape, jnp.float32), -6.0, 6.0)
    return values.astype(jnp.bfloat16)


def draw_block_tables(key, part):
    key = jax.random.fold_in(key, 13)
    group_keys = jax.random.split(key, AROWS // AR_DEV)
    orders = jax.vmap(lambda single: jax.random.permutation(single, POOL))(group_keys)
    return orders.reshape(AROWS, MAXBLK).astype(jnp.int32)


def draw_cache_lengths(key, part):
    key = jax.random.fold_in(key, 14)
    first, second = jax.random.split(key)
    lengths = jax.random.randint(first, (AROWS,), 3, MAXLEN + 1)
    longest = jax.random.randint(second, (), 0, AROWS)
    return jnp.where(jnp.arange(AROWS) == longest, MAXLEN, lengths).astype(jnp.int32)


def draw_tokens(key, part):
    key = jax.random.fold_in(key, 15)
    base_key, row_key, col_key = jax.random.split(key, 3)
    row_scale = jnp.exp(jax.random.uniform(row_key, (MROWS, 1), jnp.float32, 0.0, math.log(10.0)))
    col_scale = jnp.exp(jax.random.uniform(col_key, (1, D), jnp.float32, math.log(0.3), math.log(3.0)))
    base = jnp.clip(jax.random.normal(base_key, (MROWS, D), jnp.float32), -6.0, 6.0)
    return (base * row_scale * col_scale).astype(jnp.bfloat16)


def level_of(stream_key, extent, cuts, smallest, largest):
    def one(position, blocks):
        heights = jax.random.uniform(jax.random.fold_in(jax.random.fold_in(stream_key, 6), position), (blocks,), jnp.float32, smallest / len(cuts), largest / len(cuts))
        return jnp.repeat(jnp.exp(heights), extent[position] // blocks).reshape((-1,) + (1,) * (len(extent) - position - 1))

    level = one(*cuts[0])
    for cut in cuts[1:]:
        level = level * one(*cut)
    return level


def routed_block(key, own, number, rows, amount, top, reach, skew):
    sequence = jax.random.permutation(key, amount)
    crowded, usual = portions_of(amount, rows * top, reach, skew, True), portions_of(amount, rows * top, reach, skew, False)
    places = jnp.arange(amount)

    def named(sizes, offset_by):
        used = int((sizes > 0).sum())
        fixed = max(1, used // 4)
        passed = fixed + (places - fixed + offset_by * (used - fixed)) % max(1, amount - fixed)
        return jnp.zeros((amount,), jnp.int32).at[sequence[jnp.where(places < fixed, places, passed)]].set(jnp.asarray(sizes, jnp.int32))

    sizes = jnp.where(number % 4 == 0, named(crowded, number // 4), named(usual, number - number // 4 - 1))
    mixed = jax.random.permutation(jax.random.fold_in(own, 3), amount)
    giver, receiver = mixed[0:amount // 2 * 2:2], mixed[1:amount // 2 * 2:2]
    margin = jnp.minimum(sizes[giver] - 1, reach - sizes[receiver]) // 2
    margin = jnp.where((giver == sequence[0]) | (receiver == sequence[0]) | (sizes[receiver] == 0), 0, jnp.maximum(margin, 0))
    passed = jax.random.randint(jax.random.fold_in(own, 4), (amount // 2,), 0, 1 << 20) % (margin + 1)
    sizes = sizes.at[giver].add(-passed).at[receiver].add(passed)
    members = jnp.searchsorted(jnp.cumsum(sizes), jnp.arange(rows * top), side="right").astype(jnp.int32)
    table = members.reshape(top, rows).T
    table = table[jax.random.permutation(jax.random.fold_in(own, 1), rows)]
    offset_by = jax.random.randint(jax.random.fold_in(own, 2), (rows, 1), 0, top)
    return jnp.take_along_axis(table, (jnp.arange(top)[None, :] + offset_by) % top, axis=1)


def portions_of(number_of, total, most, lean, full):
    portions = [(1 << 20) // math.isqrt(rank ** lean) + 1 for rank in range(1, number_of + 1)]
    largest = most if full else min(most, max(-(-total // number_of), total * portions[0] // sum(portions)))
    least = 1 if total - largest >= number_of - 1 else 0
    holding, surplus = [largest] + [least] * (number_of - 1), total - largest - least * (number_of - 1)
    while surplus > 0:
        free = [i for i in range(1, number_of) if holding[i] < largest] or [i for i in range(1, number_of) if holding[i] < most]
        whole, left = sum([portions[i] for i in free]), surplus
        for i in free:
            more = min(most - holding[i], max(1, left * portions[i] // whole), surplus)
            holding[i] = holding[i] + more
            surplus = surplus - more
    return np.array(holding)


def noise(key, extent, width, limit, cuts=(), held_as=jnp.bfloat16):
    values = width * jax.random.normal(key, extent, jnp.float32)
    if cuts:
        values = values * level_of(key, extent, cuts, -0.22, 0.18)
    return jnp.clip(values, -limit, limit).astype(held_as)


def setup_inputs(seed: int = 0, part: int = 0) -> dict:
    splits = jax.random.split(jax.random.key(seed), 13)
    own_keys = jax.random.split(jax.random.fold_in(splits[12], part), 13)
    queries = draw_queries(jax.random.fold_in(jax.random.fold_in(splits[12], part), 71), part)
    new_keys = noise(own_keys[1], (AROWS, KVH, HD), 1.0, 6.0, ((0, 8), (1, 2)))
    new_values = noise(own_keys[2], (AROWS, KVH, HD), 1.0, 6.0, ((0, 8), (1, 2)))
    kv_cache = draw_kv_cache(jax.random.fold_in(jax.random.fold_in(splits[12], part), 71), part)
    block_tables = draw_block_tables(jax.random.fold_in(jax.random.fold_in(splits[12], part), 71), part)
    cache_lengths = draw_cache_lengths(jax.random.fold_in(jax.random.fold_in(splits[12], part), 71), part)
    tokens = draw_tokens(jax.random.fold_in(jax.random.fold_in(splits[12], part), 71), part)
    gain = jnp.clip(1.0 + 0.1 * jax.random.normal(splits[7], (D,), jnp.float32), 0.5, 1.5)
    expert_ids_keys = jax.random.split(jax.random.fold_in(own_keys[8], 1), MROWS // MROWS_DEV)
    expert_ids_turns = jax.random.permutation(jax.random.fold_in(own_keys[8], 3), MROWS // MROWS_DEV)
    expert_ids = jax.vmap(lambda own, number: routed_block(jax.random.fold_in(own_keys[8], 2), own, number, MROWS_DEV, EXPERTS, TOP, MOST, 2))(expert_ids_keys, expert_ids_turns).reshape((MROWS, TOP))
    gate_weights = jnp.clip(jnp.exp(math.log(1.0) - 2.9957323 * jax.random.uniform(own_keys[9], (MROWS, TOP), jnp.float32) ** level_of(own_keys[9], (MROWS, TOP), ((0, 16),), -0.2, 0.2)), 0.05, 1.0)
    w_in = noise(splits[10], (EXPERTS * SLICES, 2, UNITS, D), D ** -0.5, 0.125, ((0, 16),))
    w_out = noise(splits[11], (EXPERTS * SLICES, UNITS, D), FF ** -0.5, 0.15625, ((0, 16),))
    return {"queries": queries, "new_keys": new_keys, "new_values": new_values, "kv_cache": kv_cache, "block_tables": block_tables, "cache_lengths": cache_lengths, "tokens": tokens, "gain": gain, "expert_ids": expert_ids, "gate_weights": gate_weights, "w_in": w_in, "w_out": w_out}


epsilon = 1e-06

def attend_row(operands, kv_cache):
    grouped, key_new, value_new, table, length, base = operands
    pages = kv_cache[table + base]
    pages = pages.reshape(MAXLEN, 2, KVH, HD)
    keys = pages[:, 0].astype(jnp.float32)
    values = pages[:, 1].astype(jnp.float32)
    query = grouped.astype(jnp.float32)
    scale = HD ** (-0.5)
    scores = jnp.einsum('kgd,lkd->kgl', query, keys) * scale
    inside = jnp.arange(MAXLEN, dtype=jnp.int32) < length
    scores = jnp.where(inside[None, None, :], scores, -jnp.inf)
    own = jnp.einsum('kgd,kd->kg', query, key_new.astype(jnp.float32)) * scale
    top = jnp.maximum(lax.optimization_barrier(jnp.max(scores, axis=2)), own)
    weights = jnp.exp(scores - top[:, :, None])
    own_weight = jnp.exp(own - top)
    total = lax.optimization_barrier(jnp.sum(weights, axis=2)) + own_weight
    probs = (weights / total[:, :, None]).astype(jnp.bfloat16)
    own_prob = (own_weight / total).astype(jnp.bfloat16)
    mixed = jnp.einsum('kgl,lkd->kgd', probs.astype(jnp.float32), values)
    mixed = mixed + own_prob.astype(jnp.float32)[:, :, None] * value_new.astype(jnp.float32)[:, None, :]
    return mixed.astype(jnp.bfloat16).reshape(HQ, HD)

def run_expert(operands):
    rows_in, weights_in, weights_out = operands
    floats = rows_in.astype(jnp.float32)
    both = jnp.einsum('nd,sgud->sgnu', floats, weights_in.astype(jnp.float32))
    hidden = (jax.nn.silu(both[:, 0]) * both[:, 1]).astype(jnp.bfloat16)
    parts = jnp.einsum('snu,sud->snd', hidden.astype(jnp.float32), weights_out.astype(jnp.float32)).astype(jnp.bfloat16)
    return lax.optimization_barrier(jnp.sum(parts.astype(jnp.float32), axis=0)).astype(jnp.bfloat16)

def mix_experts(tokens, gain, expert_ids, gate_weights, w_in, w_out):
    rows = tokens.shape[0]
    senders = rows // MROWS_DEV
    floats = tokens.astype(jnp.float32)
    normed = (floats * lax.rsqrt(lax.optimization_barrier(jnp.mean(floats * floats, axis=1, keepdims=True)) + epsilon) * gain).astype(jnp.bfloat16)
    chosen = expert_ids.reshape(senders, MROWS_DEV * TOP)
    onehot = (chosen[:, :, None] == jnp.arange(EXPERTS, dtype=jnp.int32)[None, None, :]).astype(jnp.int32)
    earlier = jnp.cumsum(onehot, axis=1) - onehot
    slots = lax.optimization_barrier(jnp.sum(earlier * onehot, axis=2))
    sender = jnp.arange(senders, dtype=jnp.int32)[:, None]
    places = ((chosen * senders + sender) * MOST + slots).astype(jnp.int32)
    places = places.reshape(rows, TOP)
    sources = jnp.repeat(jnp.arange(rows, dtype=jnp.int32), TOP)
    buckets = jnp.zeros((EXPERTS * senders * MOST, D), jnp.bfloat16)
    buckets = buckets.at[places.reshape(-1)].set(normed[sources])
    buckets = buckets.reshape(EXPERTS, senders * MOST, D)
    outputs = lax.map(run_expert, (buckets, w_in.reshape(EXPERTS, SLICES, 2, UNITS, D), w_out.reshape(EXPERTS, SLICES, UNITS, D)))
    flat_out = outputs.reshape(EXPERTS * senders * MOST, D)
    shares = gate_weights / lax.optimization_barrier(jnp.sum(gate_weights, axis=1, keepdims=True))
    mixed = jnp.zeros((rows, D), jnp.float32)
    for column in range(TOP):
        mixed = mixed + shares[:, column:column + 1] * flat_out[places[:, column]].astype(jnp.float32)
    return mixed.astype(jnp.bfloat16)

def reference(queries, new_keys, new_values, kv_cache, block_tables, cache_lengths, tokens, gain, expert_ids, gate_weights, w_in, w_out):
    rows = queries.shape[0]
    grouped = queries.reshape(rows, KVH, HQ // KVH, HD)
    bases = (jnp.arange(rows, dtype=jnp.int32) // AR_DEV * POOL).astype(jnp.int32)
    attn_out = lax.map(partial(attend_row, kv_cache=kv_cache), (grouped, new_keys, new_values, block_tables, cache_lengths, bases))
    moe_out = mix_experts(tokens, gain, expert_ids, gate_weights, w_in, w_out)
    return (attn_out, moe_out)
```

```python
import functools

import jax
import jax.numpy as jnp
from jax import lax
from jax.experimental import pallas as pl
from jax.experimental.pallas import tpu as pltpu
from jax.sharding import PartitionSpec as P

TOP = 8
EXP_RANK = 4


epsilon = 1e-06
MESH = pl.DeviceIdType.MESH
K_PARTS = 4
J_PARTS = 4
UNIT_TILE = 512
LOW = 64
NT = (((1,), (1,)), ((), ()))


def dot(a, b):
    return jnp.dot(a, b, preferred_element_type=jnp.float32)


def dot_nt(a, b):
    return lax.dot_general(a, b, NT, preferred_element_type=jnp.float32)


def attend_block(table, length, q, new_k, new_v, kv, out):
    heads, size = q.shape
    kv_heads = new_k.shape[0]
    pages = table.shape[1]
    columns = kv.shape[0]
    page_len = columns // (pages * 2 * kv_heads)
    per = heads // kv_heads
    scale = size ** (-0.5)
    col = lax.broadcasted_iota(jnp.int32, (heads, columns), 1)
    head = lax.broadcasted_iota(jnp.int32, (heads, columns), 0)
    token = lax.div(col, 2 * kv_heads)
    inner = col - token * (2 * kv_heads)
    page = lax.div(token, page_len)
    slot = token - page * page_len
    place = jnp.zeros_like(col)
    for p in range(pages):
        order = jnp.int32(0)
        for j in range(pages):
            order = order + jnp.where(table[0, j] == p, j, 0)
        place = jnp.where(page == p, order * page_len + slot, place)
    valid = (inner == lax.div(head, per)) & (place < length[0])
    qv = q[...]
    kvv = kv[...]
    scores = jnp.where(valid, dot_nt(qv, kvv) * scale, -1e30)
    row = lax.broadcasted_iota(jnp.int32, (heads, size), 0)
    key = jnp.zeros((heads, size), jnp.float32)
    value = jnp.zeros((heads, size), jnp.float32)
    for g in range(kv_heads):
        mine = lax.div(row, per) == g
        key = jnp.where(mine, new_k[g : g + 1, :].astype(jnp.float32), key)
        value = jnp.where(mine, new_v[g : g + 1, :].astype(jnp.float32), value)
    own = jnp.sum(qv.astype(jnp.float32) * key, axis=1, keepdims=True) * scale
    top = jnp.maximum(jnp.max(scores, axis=1, keepdims=True), own)
    weights = jnp.where(valid, jnp.exp(scores - top), 0.0)
    own_weight = jnp.exp(own - top)
    total = jnp.sum(weights, axis=1, keepdims=True) + own_weight
    probs = pltpu.roll(weights / total, kv_heads, 1).astype(jnp.bfloat16)
    own_prob = (own_weight / total).astype(jnp.bfloat16).astype(jnp.float32)
    out[...] = (dot(probs, kvv) + own_prob * value).astype(out.dtype)


def layer_kernel(
    table, length, q, new_k, new_v, kv_hbm, tokens, gain, ids, gates, win_hbm, wout_hbm,
    attn_out, moe_out,
    kv, win, wout, xg, mg, grid_in, grid_out, acc, hid, pj, ybuf, r1, s2, r2, s3, r3, keep,
    local_sem, send_sem, gather_sem, r1_sem, r2_sem, r3_sem,
):
    z, x, c = lax.axis_index("expert"), lax.axis_index("attn"), lax.axis_index("tp")
    ranks = lax.axis_size("expert")
    rows, width = tokens.shape
    devices = ranks * 4
    total_rows = devices * rows
    kc = width // K_PARTS
    wj = width // J_PARTS
    units = wout.shape[0]
    slots = grid_in.shape[0]
    choices = ids.shape[1]

    def place_of(zz, xx, cc):
        return (cc * 2 + xx) * ranks + zz

    me = place_of(z, x, c)
    expert = (z * 2 + x) * 2 + c
    to_core, to_x = {"tp": 1 - c}, {"attn": 1 - x}
    z_next = [lax.rem(z + d, ranks) for d in range(1, ranks)]
    z_prev = [lax.rem(z + ranks - d, ranks) for d in range(1, ranks)]
    peers = [to_core, to_x] + [{"expert": zz} for zz in z_next]

    barrier = pltpu.get_barrier_semaphore()
    for peer in peers:
        pl.semaphore_signal(barrier, inc=1, device_id=peer, device_id_type=MESH)

    local = []

    def load(src, dst):
        copy = pltpu.make_async_copy(src, dst, local_sem.at[len(local)])
        copy.start()
        local.append(copy)

    load(kv_hbm, kv)
    in_tiles = win.shape[0] // UNIT_TILE
    for n in range(in_tiles):
        part = pl.ds(n * UNIT_TILE, UNIT_TILE)
        load(win_hbm.at[part], win.at[part])
    for n in range(units // UNIT_TILE):
        part = pl.ds(n * UNIT_TILE, UNIT_TILE)
        load(wout_hbm.at[part], wout.at[part])

    share = gates[...] / jnp.sum(gates[...], axis=1, keepdims=True)
    high = share.astype(jnp.bfloat16).astype(jnp.float32)
    low = share - high
    lane = lax.broadcasted_iota(jnp.int32, (rows, 2 * LOW), 1)
    meta = jnp.zeros((rows, 2 * LOW), jnp.float32)
    chosen = ids[...]
    for k in range(choices):
        one = chosen[:, k : k + 1]
        meta = jnp.where(lane == one, high[:, k : k + 1], meta)
        meta = jnp.where(lane == one + LOW, low[:, k : k + 1], meta)
    mg[me] = meta.astype(jnp.bfloat16)
    floats = tokens[...].astype(jnp.float32)
    normed = floats * lax.rsqrt(jnp.mean(floats * floats, axis=1, keepdims=True) + epsilon)
    normed = (normed * gain[...]).astype(jnp.bfloat16)
    for k in range(K_PARTS):
        xg[k, me] = normed[:, k * kc : (k + 1) * kc]

    pl.semaphore_wait(barrier, len(peers))
    sent = []

    def push(src, dst, recv, peer):
        copy = pltpu.make_async_remote_copy(
            src_ref=src, dst_ref=dst, send_sem=send_sem.at[len(sent)], recv_sem=recv,
            device_id=peer, device_id_type=MESH,
        )
        copy.start()
        sent.append(copy)

    def arrived(ref, recv):
        pltpu.make_async_remote_copy(
            src_ref=ref, dst_ref=ref, send_sem=send_sem.at[0], recv_sem=recv,
            device_id=to_core, device_id_type=MESH,
        ).wait_recv()

    def block(k, at):
        return mg.at[at] if k == 0 else xg.at[k - 1, at]

    def give(k, at, peer):
        push(block(k, at), block(k, at), gather_sem.at[k, at], peer)

    def take(k, at):
        arrived(block(k, at), gather_sem.at[k, at])

    def own_out(k):
        give(k, me, to_x)
        for zz in z_next:
            give(k, me, {"expert": zz})
        give(k, me, to_core)

    def along_z(k):
        for zz in z_prev:
            at = place_of(zz, x, c)
            take(k, at)
            give(k, at, to_x)
            give(k, at, to_core)

    def along_x(k):
        for zz in [z] + z_prev:
            at = place_of(zz, 1 - x, c)
            take(k, at)
            give(k, at, to_core)

    def along_core(k):
        for xx in (x, 1 - x):
            for zz in [z] + z_prev:
                take(k, place_of(zz, xx, 1 - c))

    for k in range(K_PARTS + 1):
        own_out(k)
    local[0].wait()
    attend_block(table, length, q, new_k, new_v, kv, attn_out)
    r_row = lax.broadcasted_iota(jnp.int32, (total_rows, total_rows), 0)
    r_col = lax.broadcasted_iota(jnp.int32, (total_rows, total_rows), 1)
    before = jnp.where(r_row > r_col, 1.0, 0.0).astype(jnp.bfloat16)
    after = jnp.where(r_row < r_col, 1.0, 0.0).astype(jnp.bfloat16)
    pj[...] = jnp.zeros_like(pj)
    along_z(0)
    along_z(1)
    along_x(0)
    along_core(0)

    routes = mg[...].reshape(total_rows, 2 * LOW)
    named = jnp.where(routes.astype(jnp.float32) > 0.0, 1.0, 0.0)
    lanes = lax.broadcasted_iota(jnp.int32, (total_rows, 2 * LOW), 1)
    named = jnp.where(lanes == expert, named, 0.0)
    named_b = named.astype(jnp.bfloat16)
    m_col = jnp.sum(named, axis=1, keepdims=True)
    at_col = jnp.sum(dot(before, named_b), axis=1, keepdims=True)
    ones = jnp.ones((16, 2 * LOW), jnp.bfloat16)
    m_row = dot_nt(ones, named_b)
    at_row = dot(m_row.astype(jnp.bfloat16), after)
    s_row = lax.broadcasted_iota(jnp.int32, (slots, total_rows), 0).astype(jnp.float32)
    grid_in[...] = jnp.where(
        (s_row == at_row[0:1, :]) & (m_row[0:1, :] > 0.5), 1.0, 0.0
    ).astype(jnp.bfloat16)
    s_col = lax.broadcasted_iota(jnp.int32, grid_out.shape, 1).astype(jnp.float32)
    grid_out[...] = jnp.where((s_col == at_col) & (m_col > 0.5), 1.0, 0.0).astype(jnp.bfloat16)
    picked = dot(grid_in[...], routes)
    p_lane = lax.broadcasted_iota(jnp.int32, (slots, 2 * LOW), 1)
    slot_share = jnp.sum(
        jnp.where((p_lane == expert) | (p_lane == expert + LOW), picked, 0.0), axis=1, keepdims=True
    )
    along_x(1)

    for copy in local[1:]:
        copy.wait()
    for k in range(K_PARTS):
        if k + 1 < K_PARTS:
            along_z(k + 2)
        along_core(k + 1)
        rows_in = dot(grid_in[...], xg[k].reshape(total_rows, kc)).astype(jnp.bfloat16)

        def tile(n, _, k=k, rows_in=rows_in):
            start = pl.multiple_of(n * UNIT_TILE, UNIT_TILE)
            product = dot_nt(rows_in, win[pl.ds(start, UNIT_TILE), k * kc : (k + 1) * kc])
            acc[n] = product if k == 0 else acc[n] + product
            return 0

        lax.fori_loop(0, in_tiles, tile, 0)
        if k + 1 < K_PARTS:
            along_x(k + 2)

    for n in range(in_tiles // 2):
        gate = acc[n]
        hid[:, n * UNIT_TILE : (n + 1) * UNIT_TILE] = (
            gate / (1.0 + jnp.exp(-gate)) * acc[n + in_tiles // 2]
        ).astype(jnp.bfloat16)

    half = grid_out.shape[0] // 2

    def first(j):
        part = dot(hid[...], wout[:, j * wj : (j + 1) * wj]) * slot_share
        pj[0:slots, :] = part.astype(jnp.bfloat16)
        for cc in (1 - c, c):
            spread = dot(grid_out[pl.ds(pl.multiple_of(cc * half, half), half), :], pj[...])
            ybuf[j, cc] = spread.astype(jnp.bfloat16).reshape(2, half // 2, wj)
            if cc is not c:
                push(ybuf.at[j, cc], r1.at[j], r1_sem.at[j], to_core)

    def second(j):
        arrived(r1.at[j], r1_sem.at[j])
        s2[j] = (
            ybuf[j, c, 1 - x].astype(jnp.float32) + r1[j, 1 - x].astype(jnp.float32)
        ).astype(jnp.bfloat16)
        push(s2.at[j], r2.at[j], r2_sem.at[j], to_x)

    def third(j):
        arrived(r2.at[j], r2_sem.at[j])
        for zz in z_next + [z]:
            part = pl.ds(pl.multiple_of(zz * rows, rows), rows)
            value = (
                ybuf[j, c, x, part, :].astype(jnp.float32)
                + r1[j, x, part, :].astype(jnp.float32)
                + r2[j, part, :].astype(jnp.float32)
            )
            if zz is z:
                keep[j] = value
            else:
                s3[j, zz] = value.astype(jnp.bfloat16)
                push(s3.at[j, zz], r3.at[j, z], r3_sem.at[j, z], {"expert": zz})

    def fourth(j):
        value = keep[j]
        for zz in z_prev:
            arrived(r3.at[j, zz], r3_sem.at[j, zz])
            value = value + r3[j, zz].astype(jnp.float32)
        moe_out[:, j * wj : (j + 1) * wj] = value.astype(moe_out.dtype)

    for j in range(J_PARTS):
        first(j)
        if j:
            second(j - 1)
    second(J_PARTS - 1)
    for j in range(J_PARTS):
        third(j)
        if j:
            fourth(j - 1)
    fourth(J_PARTS - 1)
    for copy in sent:
        copy.wait_send()


def fused_layer(
    queries, new_keys, new_values, kv_cache, block_tables, cache_lengths,
    tokens, gain, expert_ids, gate_weights, w_in, w_out,
):
    rows, width = tokens.shape
    ranks = lax.axis_size("expert")
    devices = 4 * ranks
    experts = devices
    most = max(2, rows * TOP // experts + 1)
    slots = -(-most * devices // 16) * 16
    padded = -(-slots // 128) * 128
    units = w_out.shape[1]
    total = devices * rows
    kc, wj = width // K_PARTS, width // J_PARTS
    heads, size = queries.shape[1:]
    bf, f32 = jnp.bfloat16, jnp.float32
    kv = kv_cache.reshape(-1, size)
    sends = 15 * (K_PARTS + 1) + (2 + ranks - 1) * J_PARTS
    vmem = pl.BlockSpec(memory_space=pltpu.VMEM)
    smem = pl.BlockSpec(memory_space=pltpu.SMEM)
    anyw = pl.BlockSpec(memory_space=pl.ANY)
    attn_out, moe_out = pl.pallas_call(
        layer_kernel,
        out_shape=(
            jax.ShapeDtypeStruct((heads, size), bf),
            jax.ShapeDtypeStruct((rows, width), bf),
        ),
        in_specs=[smem, smem, vmem, vmem, vmem, anyw, vmem, vmem, vmem, vmem, anyw, anyw],
        out_specs=(vmem, vmem),
        scratch_shapes=[
            pltpu.VMEM(kv.shape, bf),
            pltpu.VMEM((2 * units, width), bf),
            pltpu.VMEM((units, width), bf),
            pltpu.VMEM((K_PARTS, devices, rows, kc), bf),
            pltpu.VMEM((devices, rows, 2 * LOW), bf),
            pltpu.VMEM((slots, total), bf),
            pltpu.VMEM((total, padded), bf),
            pltpu.VMEM((2 * units // UNIT_TILE, slots, UNIT_TILE), f32),
            pltpu.VMEM((slots, units), bf),
            pltpu.VMEM((padded, wj), bf),
            pltpu.VMEM((J_PARTS, 2, 2, total // 4, wj), bf),
            pltpu.VMEM((J_PARTS, 2, total // 4, wj), bf),
            pltpu.VMEM((J_PARTS, total // 4, wj), bf),
            pltpu.VMEM((J_PARTS, total // 4, wj), bf),
            pltpu.VMEM((J_PARTS, ranks, rows, wj), bf),
            pltpu.VMEM((J_PARTS, ranks, rows, wj), bf),
            pltpu.VMEM((J_PARTS, rows, wj), f32),
            pltpu.SemaphoreType.DMA((1 + 3 * units // UNIT_TILE,)),
            pltpu.SemaphoreType.DMA((sends,)),
            pltpu.SemaphoreType.DMA((K_PARTS + 1, devices)),
            pltpu.SemaphoreType.DMA((J_PARTS,)),
            pltpu.SemaphoreType.DMA((J_PARTS,)),
            pltpu.SemaphoreType.DMA((J_PARTS, ranks)),
        ],
        compiler_params=pltpu.CompilerParams(
            collective_id=0, has_side_effects=True, vmem_limit_bytes=56 * 1024 * 1024
        ),
    )(
        block_tables, cache_lengths, queries[0], new_keys[0], new_values[0], kv,
        tokens, gain.reshape(1, width), expert_ids, gate_weights,
        w_in.reshape(2 * units, width), w_out.reshape(units, width),
    )
    return (attn_out.reshape(1, heads, size), moe_out)


def attend(queries, new_keys, new_values, kv_cache, block_tables, cache_lengths):
    rows, heads, size = queries.shape
    kv_heads = new_keys.shape[1]
    grouped = queries.reshape(rows, kv_heads, heads // kv_heads, size)
    pages = kv_cache[block_tables]
    span = pages.shape[1] * pages.shape[2]
    pages = pages.reshape(rows, span, 2, kv_heads, size)
    scale = size ** (-0.5)
    scores = (
        jnp.einsum("rkgd,rlkd->rkgl", grouped, pages[:, :, 0], preferred_element_type=jnp.float32)
        * scale
    )
    inside = jnp.arange(span, dtype=jnp.int32)[None, :] < cache_lengths[:, None]
    scores = jnp.where(inside[:, None, None, :], scores, -jnp.inf)
    own = jnp.einsum("rkgd,rkd->rkg", grouped, new_keys, preferred_element_type=jnp.float32) * scale
    top = jnp.maximum(jnp.max(scores, axis=3), own)
    weights = jnp.exp(scores - top[..., None])
    own_weight = jnp.exp(own - top)
    total = jnp.sum(weights, axis=3) + own_weight
    probs = (weights / total[..., None]).astype(jnp.bfloat16)
    own_prob = (own_weight / total).astype(jnp.bfloat16)
    mixed = jnp.einsum("rkgl,rlkd->rkgd", probs, pages[:, :, 1], preferred_element_type=jnp.float32)
    mixed = (
        mixed
        + own_prob.astype(jnp.float32)[..., None] * new_values.astype(jnp.float32)[:, :, None, :]
    )
    return mixed.astype(jnp.bfloat16).reshape(rows, heads, size)


def expert_part(rows_in, weights_in, weights_out):
    both = jnp.einsum("nd,gud->gnu", rows_in, weights_in, preferred_element_type=jnp.float32)
    hidden = (jax.nn.silu(both[0]) * both[1]).astype(jnp.bfloat16)
    return jnp.dot(hidden, weights_out, preferred_element_type=jnp.float32).astype(jnp.bfloat16)


def per_device(
    queries,
    new_keys,
    new_values,
    kv_cache,
    block_tables,
    cache_lengths,
    tokens,
    gain,
    expert_ids,
    gate_weights,
    w_in,
    w_out,
):
    ranks, cores = lax.axis_size("expert"), lax.axis_size("tp")
    fits = ranks * 4 * tokens.shape[0] <= 512 and queries.shape[0] == 1
    if lax.axis_size("attn") == 2 and cores == 2 and fits:
        return fused_layer(
            queries, new_keys, new_values, kv_cache, block_tables, cache_lengths,
            tokens, gain, expert_ids, gate_weights, w_in, w_out,
        )
    attn_out = attend(queries, new_keys, new_values, kv_cache, block_tables, cache_lengths)
    rows, width = tokens.shape
    ranks = lax.axis_size("expert")
    peers = lax.axis_size(("attn", "tp"))
    slices = peers // EXP_RANK
    experts = EXP_RANK * ranks
    most = max(2, rows * TOP // experts + 1)
    floats = tokens.astype(jnp.float32)
    normed = (
        floats * lax.rsqrt(jnp.mean(floats * floats, axis=1, keepdims=True) + epsilon) * gain
    ).astype(jnp.bfloat16)
    chosen = expert_ids.reshape(-1)
    onehot = (chosen[:, None] == jnp.arange(experts, dtype=jnp.int32)[None, :]).astype(jnp.int32)
    earlier = jnp.cumsum(onehot, axis=0) - onehot
    targets = chosen * most + jnp.sum(earlier * onehot, axis=1)
    picks = (jnp.arange(experts * most, dtype=jnp.int32)[:, None] == targets[None, :]).astype(
        jnp.int32
    )
    picks = jnp.sum(picks.reshape(experts * most, rows, TOP), axis=2).astype(jnp.bfloat16)
    buckets = jnp.dot(picks, normed, preferred_element_type=jnp.float32).astype(jnp.bfloat16)
    buckets = buckets.reshape(experts, most, width)
    grouped = buckets.reshape(ranks, EXP_RANK, most, width)
    copies = jnp.repeat(grouped, slices, axis=1)
    in_rank = lax.all_to_all(copies, ("attn", "tp"), split_axis=1, concat_axis=1, tiled=True)
    arrived = lax.all_to_all(in_rank, "expert", split_axis=0, concat_axis=0, tiled=True)
    partial_rows = expert_part(arrived.reshape(-1, width), w_in[0], w_out[0])
    partial_rows = partial_rows.reshape(ranks, peers, most, width)
    returned = lax.all_to_all(partial_rows, "expert", split_axis=0, concat_axis=0, tiled=True)
    gathered = lax.all_to_all(returned, ("attn", "tp"), split_axis=1, concat_axis=1, tiled=True)
    summed = jnp.sum(
        gathered.reshape(ranks, EXP_RANK, slices, most, width).astype(jnp.float32), axis=2
    )
    home = summed.astype(jnp.bfloat16).reshape(experts, most, width)
    flat_home = home.reshape(experts * most, width)
    shares = gate_weights / jnp.sum(gate_weights, axis=1, keepdims=True)
    placed = targets.reshape(rows, TOP)
    mixed = jnp.zeros((rows, width), jnp.float32)
    for column in range(TOP):
        mixed = mixed + shares[:, column : column + 1] * flat_home[placed[:, column]].astype(
            jnp.float32
        )
    return (attn_out, mixed.astype(jnp.bfloat16))


def solution(mesh):
    return jax.shard_map(
        per_device,
        mesh=mesh,
        in_specs=(
            P(("groups", "expert", "attn"), "tp", None),
            P(("groups", "expert", "attn"), "tp", None),
            P(("groups", "expert", "attn"), "tp", None),
            P(("groups", "expert", "attn"), None, None, "tp", None),
            P(("groups", "expert", "attn"), None),
            P(("groups", "expert", "attn")),
            P(("groups", "expert", "attn", "tp"), None),
            P(),
            P(("groups", "expert", "attn", "tp"), None),
            P(("groups", "expert", "attn", "tp"), None),
            P(("expert", "attn", "tp"), None, None, None),
            P(("expert", "attn", "tp"), None, None),
        ),
        out_specs=(
            P(("groups", "expert", "attn"), "tp", None),
            P(("groups", "expert", "attn", "tp"), None),
        ),
        check_vma=False,
    )
```

```python
import functools

import jax
import jax.numpy as jnp
from jax import lax
from jax.experimental import pallas as pl
from jax.experimental.pallas import tpu as pltpu
from jax.sharding import PartitionSpec as P

TOP = 8
EXP_RANK = 4


epsilon = 1e-06
MESH = pl.DeviceIdType.MESH
K_PARTS = 2
J_PARTS = 4
UNIT_TILE = 768
LOW = 64
NT = (((1,), (1,)), ((), ()))


def dot(a, b):
    return jnp.dot(a, b, preferred_element_type=jnp.float32)


def dot_nt(a, b):
    return lax.dot_general(a, b, NT, preferred_element_type=jnp.float32)


def attend_block(table, length, q, new_k, new_v, kv, out):
    heads, size = q.shape
    kv_heads = new_k.shape[0]
    pages = table.shape[1]
    columns = kv.shape[0]
    page_len = columns // (pages * 2 * kv_heads)
    per = heads // kv_heads
    scale = size ** (-0.5)
    col = lax.broadcasted_iota(jnp.int32, (heads, columns), 1)
    head = lax.broadcasted_iota(jnp.int32, (heads, columns), 0)
    token = lax.div(col, 2 * kv_heads)
    inner = col - token * (2 * kv_heads)
    page = lax.div(token, page_len)
    slot = token - page * page_len
    place = jnp.zeros_like(col)
    for p in range(pages):
        order = jnp.int32(0)
        for j in range(pages):
            order = order + jnp.where(table[0, j] == p, j, 0)
        place = jnp.where(page == p, order * page_len + slot, place)
    valid = (inner == lax.div(head, per)) & (place < length[0])
    qv = q[...]
    kvv = kv[...]
    scores = jnp.where(valid, dot_nt(qv, kvv) * scale, -1e30)
    row = lax.broadcasted_iota(jnp.int32, (heads, size), 0)
    key = jnp.zeros((heads, size), jnp.float32)
    value = jnp.zeros((heads, size), jnp.float32)
    for g in range(kv_heads):
        mine = lax.div(row, per) == g
        key = jnp.where(mine, new_k[g : g + 1, :].astype(jnp.float32), key)
        value = jnp.where(mine, new_v[g : g + 1, :].astype(jnp.float32), value)
    own = jnp.sum(qv.astype(jnp.float32) * key, axis=1, keepdims=True) * scale
    top = jnp.maximum(jnp.max(scores, axis=1, keepdims=True), own)
    weights = jnp.where(valid, jnp.exp(scores - top), 0.0)
    own_weight = jnp.exp(own - top)
    total = jnp.sum(weights, axis=1, keepdims=True) + own_weight
    probs = pltpu.roll(weights / total, kv_heads, 1).astype(jnp.bfloat16)
    own_prob = (own_weight / total).astype(jnp.bfloat16).astype(jnp.float32)
    out[...] = (dot(probs, kvv) + own_prob * value).astype(out.dtype)


def layer_kernel(
    table, length, q, new_k, new_v, kv_hbm, tokens, gain, ids, gates, win_hbm, wout_hbm,
    attn_out, moe_out,
    kv, win, wout, xg, mg, grid_in, grid_out, acc, hid, pj, ybuf, r1, s2, r2, s3, r3, keep,
    local_sem, send_sem, gather_sem, r1_sem, r2_sem, r3_sem,
):
    z, x, c = lax.axis_index("expert"), lax.axis_index("attn"), lax.axis_index("tp")
    ranks = lax.axis_size("expert")
    rows, width = tokens.shape
    devices = ranks * 4
    total_rows = devices * rows
    kc = width // K_PARTS
    wj = width // J_PARTS
    units = wout.shape[0]
    slots = grid_in.shape[0]
    choices = ids.shape[0]

    def place_of(zz, xx, cc):
        return (cc * 2 + xx) * ranks + zz

    me = place_of(z, x, c)
    expert = (z * 2 + x) * 2 + c
    to_core, to_x = {"tp": 1 - c}, {"attn": 1 - x}
    z_next = [lax.rem(z + d, ranks) for d in range(1, ranks)]
    z_prev = [lax.rem(z + ranks - d, ranks) for d in range(1, ranks)]
    peers = [to_core, to_x] + [{"expert": zz} for zz in z_next]

    barrier = pltpu.get_barrier_semaphore()
    for peer in peers:
        pl.semaphore_signal(barrier, inc=1, device_id=peer, device_id_type=MESH)

    local = []

    def load(src, dst):
        copy = pltpu.make_async_copy(src, dst, local_sem.at[len(local)])
        copy.start()
        local.append(copy)

    load(kv_hbm, kv)
    in_tiles = win.shape[0] // UNIT_TILE
    for n in range(in_tiles):
        part = pl.ds(n * UNIT_TILE, UNIT_TILE)
        load(win_hbm.at[part], win.at[part])
    for n in range(units // UNIT_TILE):
        part = pl.ds(n * UNIT_TILE, UNIT_TILE)
        load(wout_hbm.at[part], wout.at[part])

    share = gates[...] / jnp.sum(gates[...], axis=0, keepdims=True)
    high = share.astype(jnp.bfloat16).astype(jnp.float32)
    low = share - high
    name = lax.broadcasted_iota(jnp.int32, (2 * LOW, rows), 0)
    meta = jnp.zeros((2 * LOW, rows), jnp.float32)
    chosen = ids[...]
    for k in range(choices):
        one = chosen[k : k + 1, :]
        meta = jnp.where(name == one, high[k : k + 1, :], meta)
        meta = jnp.where(name == one + LOW, low[k : k + 1, :], meta)
    same = lax.broadcasted_iota(jnp.int32, (rows, rows), 0) == lax.broadcasted_iota(
        jnp.int32, (rows, rows), 1
    )
    unit = jnp.where(same, 1.0, 0.0).astype(jnp.bfloat16)
    mg[me] = dot_nt(unit, meta.astype(jnp.bfloat16)).astype(jnp.bfloat16)
    floats = tokens[...].astype(jnp.float32)
    normed = floats * lax.rsqrt(jnp.mean(floats * floats, axis=1, keepdims=True) + epsilon)
    normed = (normed * gain[...]).astype(jnp.bfloat16)
    for k in range(K_PARTS):
        xg[k, me] = normed[:, k * kc : (k + 1) * kc]

    pl.semaphore_wait(barrier, len(peers))
    sent, across, used = [], [], [0]

    def push(src, dst, recv, peer):
        copy = pltpu.make_async_remote_copy(
            src_ref=src, dst_ref=dst, send_sem=send_sem.at[used[0]], recv_sem=recv,
            device_id=peer, device_id_type=MESH,
        )
        copy.start()
        used[0] += 1
        sent.append(copy)
        return copy

    def arrived(ref, recv):
        pltpu.make_async_remote_copy(
            src_ref=ref, dst_ref=ref, send_sem=send_sem.at[0], recv_sem=recv,
            device_id=to_core, device_id_type=MESH,
        ).wait_recv()

    def block(k, at):
        return mg.at[at] if k == 0 else xg.at[k - 1, at]

    def give(k, at, peer):
        push(block(k, at), block(k, at), gather_sem.at[k, at], peer)

    def take(k, at):
        arrived(block(k, at), gather_sem.at[k, at])

    def own_near(k):
        give(k, me, to_x)
        give(k, me, to_core)

    def own_far(k, i):
        give(k, me, {"expert": z_next[i]})

    def along_z(k):
        for i, zz in enumerate(z_prev):
            at = place_of(zz, x, c)
            take(k, at)
            if k and k < K_PARTS:
                own_far(k + 1, i)
            give(k, at, to_x)
            give(k, at, to_core)

    def along_x(k):
        for zz in [z] + z_prev:
            at = place_of(zz, 1 - x, c)
            take(k, at)
            give(k, at, to_core)

    def along_core(k):
        for xx in (x, 1 - x):
            for zz in [z] + z_prev:
                take(k, place_of(zz, xx, 1 - c))

    for k in range(2):
        for i in range(ranks - 1):
            own_far(k, i)
    for k in range(K_PARTS + 1):
        own_near(k)
    local[0].wait()
    attend_block(table, length, q, new_k, new_v, kv, attn_out)
    r_row = lax.broadcasted_iota(jnp.int32, (total_rows, total_rows), 0)
    r_col = lax.broadcasted_iota(jnp.int32, (total_rows, total_rows), 1)
    before = jnp.where(r_row > r_col, 1.0, 0.0).astype(jnp.bfloat16)
    after = jnp.where(r_row < r_col, 1.0, 0.0).astype(jnp.bfloat16)
    pj[...] = jnp.zeros_like(pj)
    along_z(0)
    along_z(1)
    along_x(0)
    along_core(0)

    routes = mg[...].reshape(total_rows, 2 * LOW)
    named = jnp.where(routes.astype(jnp.float32) > 0.0, 1.0, 0.0)
    lanes = lax.broadcasted_iota(jnp.int32, (total_rows, 2 * LOW), 1)
    named = jnp.where(lanes == expert, named, 0.0)
    named_b = named.astype(jnp.bfloat16)
    m_col = jnp.sum(named, axis=1, keepdims=True)
    at_col = jnp.sum(dot(before, named_b), axis=1, keepdims=True)
    ones = jnp.ones((16, 2 * LOW), jnp.bfloat16)
    m_row = dot_nt(ones, named_b)
    at_row = dot(m_row.astype(jnp.bfloat16), after)
    s_row = lax.broadcasted_iota(jnp.int32, (slots, total_rows), 0).astype(jnp.float32)
    grid_in[...] = jnp.where(
        (s_row == at_row[0:1, :]) & (m_row[0:1, :] > 0.5), 1.0, 0.0
    ).astype(jnp.bfloat16)
    s_col = lax.broadcasted_iota(jnp.int32, grid_out.shape, 1).astype(jnp.float32)
    grid_out[...] = jnp.where((s_col == at_col) & (m_col > 0.5), 1.0, 0.0).astype(jnp.bfloat16)
    picked = dot(grid_in[...], routes)
    p_lane = lax.broadcasted_iota(jnp.int32, (slots, 2 * LOW), 1)
    slot_share = jnp.sum(
        jnp.where((p_lane == expert) | (p_lane == expert + LOW), picked, 0.0), axis=1, keepdims=True
    )
    along_x(1)

    for copy in local[1:]:
        copy.wait()
    for k in range(K_PARTS):
        if k + 1 < K_PARTS:
            along_z(k + 2)
        along_core(k + 1)
        rows_in = dot(grid_in[...], xg[k].reshape(total_rows, kc)).astype(jnp.bfloat16)

        def tile(n, _, k=k, rows_in=rows_in):
            start = pl.multiple_of(n * UNIT_TILE, UNIT_TILE)
            product = dot_nt(rows_in, win[pl.ds(start, UNIT_TILE), k * kc : (k + 1) * kc])
            acc[n] = product if k == 0 else acc[n] + product
            return 0

        lax.fori_loop(0, in_tiles, tile, 0)
        if k + 1 < K_PARTS:
            along_x(k + 2)

    for n in range(in_tiles // 2):
        gate = acc[n]
        hid[:, n * UNIT_TILE : (n + 1) * UNIT_TILE] = (
            gate / (1.0 + jnp.exp(-gate)) * acc[n + in_tiles // 2]
        ).astype(jnp.bfloat16)

    half = grid_out.shape[0] // 2

    def first(j):
        part = dot(hid[...], wout[:, j * wj : (j + 1) * wj]) * slot_share
        pj[0:slots, :] = part.astype(jnp.bfloat16)
        for cc in (1 - c, c):
            spread = dot(grid_out[pl.ds(pl.multiple_of(cc * half, half), half), :], pj[...])
            ybuf[j, cc] = spread.astype(jnp.bfloat16).reshape(2, half // 2, wj)
            if cc is not c:
                push(ybuf.at[j, cc], r1.at[j], r1_sem.at[j], to_core)

    def second(j):
        arrived(r1.at[j], r1_sem.at[j])
        s2[j] = (
            ybuf[j, c, 1 - x].astype(jnp.float32) + r1[j, 1 - x].astype(jnp.float32)
        ).astype(jnp.bfloat16)
        if j:
            across[j - 1].wait_send()
        across.append(push(s2.at[j], r2.at[j], r2_sem.at[j], to_x))

    def third(j):
        arrived(r2.at[j], r2_sem.at[j])
        for zz in z_next + [z]:
            part = pl.ds(pl.multiple_of(zz * rows, rows), rows)
            value = (
                ybuf[j, c, x, part, :].astype(jnp.float32)
                + r1[j, x, part, :].astype(jnp.float32)
                + r2[j, part, :].astype(jnp.float32)
            )
            if zz is z:
                keep[j] = value
            else:
                s3[j, zz] = value.astype(jnp.bfloat16)
                push(s3.at[j, zz], r3.at[j, z], r3_sem.at[j, z], {"expert": zz})

    def fourth(j):
        value = keep[j]
        for zz in z_prev:
            arrived(r3.at[j, zz], r3_sem.at[j, zz])
            value = value + r3[j, zz].astype(jnp.float32)
        moe_out[:, j * wj : (j + 1) * wj] = value.astype(moe_out.dtype)

    for step in range(J_PARTS + 4):
        for lag, stage in ((0, first), (1, second), (2, third), (4, fourth)):
            if 0 <= step - lag < J_PARTS:
                stage(step - lag)
    for copy in sent:
        if not any(copy is early for early in across[:-1]):
            copy.wait_send()


def fused_layer(
    queries, new_keys, new_values, kv_cache, block_tables, cache_lengths,
    tokens, gain, expert_ids, gate_weights, w_in, w_out,
):
    rows, width = tokens.shape
    ranks = lax.axis_size("expert")
    devices = 4 * ranks
    experts = devices
    most = max(2, rows * TOP // experts + 1)
    slots = -(-most * devices // 16) * 16
    padded = -(-slots // 128) * 128
    units = w_out.shape[1]
    total = devices * rows
    kc, wj = width // K_PARTS, width // J_PARTS
    heads, size = queries.shape[1:]
    bf, f32 = jnp.bfloat16, jnp.float32
    kv = kv_cache.reshape(-1, size)
    sends = 15 * (K_PARTS + 1) + (2 + ranks - 1) * J_PARTS
    vmem = pl.BlockSpec(memory_space=pltpu.VMEM)
    smem = pl.BlockSpec(memory_space=pltpu.SMEM)
    anyw = pl.BlockSpec(memory_space=pl.ANY)
    attn_out, moe_out = pl.pallas_call(
        layer_kernel,
        out_shape=(
            jax.ShapeDtypeStruct((heads, size), bf),
            jax.ShapeDtypeStruct((rows, width), bf),
        ),
        in_specs=[smem, smem, vmem, vmem, vmem, anyw, vmem, vmem, vmem, vmem, anyw, anyw],
        out_specs=(vmem, vmem),
        scratch_shapes=[
            pltpu.VMEM(kv.shape, bf),
            pltpu.VMEM((2 * units, width), bf),
            pltpu.VMEM((units, width), bf),
            pltpu.VMEM((K_PARTS, devices, rows, kc), bf),
            pltpu.VMEM((devices, rows, 2 * LOW), bf),
            pltpu.VMEM((slots, total), bf),
            pltpu.VMEM((total, padded), bf),
            pltpu.VMEM((2 * units // UNIT_TILE, slots, UNIT_TILE), f32),
            pltpu.VMEM((slots, units), bf),
            pltpu.VMEM((padded, wj), bf),
            pltpu.VMEM((J_PARTS, 2, 2, total // 4, wj), bf),
            pltpu.VMEM((J_PARTS, 2, total // 4, wj), bf),
            pltpu.VMEM((J_PARTS, total // 4, wj), bf),
            pltpu.VMEM((J_PARTS, total // 4, wj), bf),
            pltpu.VMEM((J_PARTS, ranks, rows, wj), bf),
            pltpu.VMEM((J_PARTS, ranks, rows, wj), bf),
            pltpu.VMEM((J_PARTS, rows, wj), f32),
            pltpu.SemaphoreType.DMA((1 + 3 * units // UNIT_TILE,)),
            pltpu.SemaphoreType.DMA((sends,)),
            pltpu.SemaphoreType.DMA((K_PARTS + 1, devices)),
            pltpu.SemaphoreType.DMA((J_PARTS,)),
            pltpu.SemaphoreType.DMA((J_PARTS,)),
            pltpu.SemaphoreType.DMA((J_PARTS, ranks)),
        ],
        compiler_params=pltpu.CompilerParams(
            collective_id=0, has_side_effects=True, vmem_limit_bytes=56 * 1024 * 1024
        ),
    )(
        block_tables, cache_lengths, queries[0], new_keys[0], new_values[0], kv,
        tokens, gain.reshape(1, width), expert_ids.T, gate_weights.T,
        w_in.reshape(2 * units, width), w_out.reshape(units, width),
    )
    return (attn_out.reshape(1, heads, size), moe_out)


def attend(queries, new_keys, new_values, kv_cache, block_tables, cache_lengths):
    rows, heads, size = queries.shape
    kv_heads = new_keys.shape[1]
    grouped = queries.reshape(rows, kv_heads, heads // kv_heads, size)
    pages = kv_cache[block_tables]
    span = pages.shape[1] * pages.shape[2]
    pages = pages.reshape(rows, span, 2, kv_heads, size)
    scale = size ** (-0.5)
    scores = (
        jnp.einsum("rkgd,rlkd->rkgl", grouped, pages[:, :, 0], preferred_element_type=jnp.float32)
        * scale
    )
    inside = jnp.arange(span, dtype=jnp.int32)[None, :] < cache_lengths[:, None]
    scores = jnp.where(inside[:, None, None, :], scores, -jnp.inf)
    own = jnp.einsum("rkgd,rkd->rkg", grouped, new_keys, preferred_element_type=jnp.float32) * scale
    top = jnp.maximum(jnp.max(scores, axis=3), own)
    weights = jnp.exp(scores - top[..., None])
    own_weight = jnp.exp(own - top)
    total = jnp.sum(weights, axis=3) + own_weight
    probs = (weights / total[..., None]).astype(jnp.bfloat16)
    own_prob = (own_weight / total).astype(jnp.bfloat16)
    mixed = jnp.einsum("rkgl,rlkd->rkgd", probs, pages[:, :, 1], preferred_element_type=jnp.float32)
    mixed = (
        mixed
        + own_prob.astype(jnp.float32)[..., None] * new_values.astype(jnp.float32)[:, :, None, :]
    )
    return mixed.astype(jnp.bfloat16).reshape(rows, heads, size)


def expert_part(rows_in, weights_in, weights_out):
    both = jnp.einsum("nd,gud->gnu", rows_in, weights_in, preferred_element_type=jnp.float32)
    hidden = (jax.nn.silu(both[0]) * both[1]).astype(jnp.bfloat16)
    return jnp.dot(hidden, weights_out, preferred_element_type=jnp.float32).astype(jnp.bfloat16)


def per_device(
    queries,
    new_keys,
    new_values,
    kv_cache,
    block_tables,
    cache_lengths,
    tokens,
    gain,
    expert_ids,
    gate_weights,
    w_in,
    w_out,
):
    ranks, cores = lax.axis_size("expert"), lax.axis_size("tp")
    fits = ranks * 4 * tokens.shape[0] <= 512 and queries.shape[0] == 1
    if lax.axis_size("attn") == 2 and cores == 2 and fits:
        return fused_layer(
            queries, new_keys, new_values, kv_cache, block_tables, cache_lengths,
            tokens, gain, expert_ids, gate_weights, w_in, w_out,
        )
    attn_out = attend(queries, new_keys, new_values, kv_cache, block_tables, cache_lengths)
    rows, width = tokens.shape
    ranks = lax.axis_size("expert")
    peers = lax.axis_size(("attn", "tp"))
    slices = peers // EXP_RANK
    experts = EXP_RANK * ranks
    most = max(2, rows * TOP // experts + 1)
    floats = tokens.astype(jnp.float32)
    normed = (
        floats * lax.rsqrt(jnp.mean(floats * floats, axis=1, keepdims=True) + epsilon) * gain
    ).astype(jnp.bfloat16)
    chosen = expert_ids.reshape(-1)
    onehot = (chosen[:, None] == jnp.arange(experts, dtype=jnp.int32)[None, :]).astype(jnp.int32)
    earlier = jnp.cumsum(onehot, axis=0) - onehot
    targets = chosen * most + jnp.sum(earlier * onehot, axis=1)
    picks = (jnp.arange(experts * most, dtype=jnp.int32)[:, None] == targets[None, :]).astype(
        jnp.int32
    )
    picks = jnp.sum(picks.reshape(experts * most, rows, TOP), axis=2).astype(jnp.bfloat16)
    buckets = jnp.dot(picks, normed, preferred_element_type=jnp.float32).astype(jnp.bfloat16)
    buckets = buckets.reshape(experts, most, width)
    grouped = buckets.reshape(ranks, EXP_RANK, most, width)
    copies = jnp.repeat(grouped, slices, axis=1)
    in_rank = lax.all_to_all(copies, ("attn", "tp"), split_axis=1, concat_axis=1, tiled=True)
    arrived = lax.all_to_all(in_rank, "expert", split_axis=0, concat_axis=0, tiled=True)
    partial_rows = expert_part(arrived.reshape(-1, width), w_in[0], w_out[0])
    partial_rows = partial_rows.reshape(ranks, peers, most, width)
    returned = lax.all_to_all(partial_rows, "expert", split_axis=0, concat_axis=0, tiled=True)
    gathered = lax.all_to_all(returned, ("attn", "tp"), split_axis=1, concat_axis=1, tiled=True)
    summed = jnp.sum(
        gathered.reshape(ranks, EXP_RANK, slices, most, width).astype(jnp.float32), axis=2
    )
    home = summed.astype(jnp.bfloat16).reshape(experts, most, width)
    flat_home = home.reshape(experts * most, width)
    shares = gate_weights / jnp.sum(gate_weights, axis=1, keepdims=True)
    placed = targets.reshape(rows, TOP)
    mixed = jnp.zeros((rows, width), jnp.float32)
    for column in range(TOP):
        mixed = mixed + shares[:, column : column + 1] * flat_home[placed[:, column]].astype(
            jnp.float32
        )
    return (attn_out, mixed.astype(jnp.bfloat16))


def solution(mesh):
    return jax.shard_map(
        per_device,
        mesh=mesh,
        in_specs=(
            P(("groups", "expert", "attn"), "tp", None),
            P(("groups", "expert", "attn"), "tp", None),
            P(("groups", "expert", "attn"), "tp", None),
            P(("groups", "expert", "attn"), None, None, "tp", None),
            P(("groups", "expert", "attn"), None),
            P(("groups", "expert", "attn")),
            P(("groups", "expert", "attn", "tp"), None),
            P(),
            P(("groups", "expert", "attn", "tp"), None),
            P(("groups", "expert", "attn", "tp"), None),
            P(("expert", "attn", "tp"), None, None, None),
            P(("expert", "attn", "tp"), None, None),
        ),
        out_specs=(
            P(("groups", "expert", "attn"), "tp", None),
            P(("groups", "expert", "attn", "tp"), None),
        ),
        check_vma=False,
    )
```

```python
import functools

import jax
import jax.numpy as jnp
from jax import lax
from jax.experimental import pallas as pl
from jax.experimental.pallas import tpu as pltpu
from jax.sharding import PartitionSpec as P

TOP = 8
EXP_RANK = 4


epsilon = 1e-06
MESH = pl.DeviceIdType.MESH
K_PARTS = 2
J_PARTS = 4
UNIT_TILE = 768
LOW = 64
NT = (((1,), (1,)), ((), ()))


def dot(a, b):
    return jnp.dot(a, b, preferred_element_type=jnp.float32)


def dot_nt(a, b):
    return lax.dot_general(a, b, NT, preferred_element_type=jnp.float32)


def attend_block(table, length, q, new_k, new_v, kv, out):
    heads, size = q.shape
    kv_heads = new_k.shape[0]
    pages = table.shape[1]
    columns = kv.shape[0]
    page_len = columns // (pages * 2 * kv_heads)
    per = heads // kv_heads
    scale = size ** (-0.5)
    col = lax.broadcasted_iota(jnp.int32, (heads, columns), 1)
    head = lax.broadcasted_iota(jnp.int32, (heads, columns), 0)
    token = lax.div(col, 2 * kv_heads)
    inner = col - token * (2 * kv_heads)
    page = lax.div(token, page_len)
    slot = token - page * page_len
    place = jnp.zeros_like(col)
    for p in range(pages):
        order = jnp.int32(0)
        for j in range(pages):
            order = order + jnp.where(table[0, j] == p, j, 0)
        place = jnp.where(page == p, order * page_len + slot, place)
    valid = (inner == lax.div(head, per)) & (place < length[0])
    qv = q[...]
    kvv = kv[...]
    scores = jnp.where(valid, dot_nt(qv, kvv) * scale, -1e30)
    row = lax.broadcasted_iota(jnp.int32, (heads, size), 0)
    key = jnp.zeros((heads, size), jnp.float32)
    value = jnp.zeros((heads, size), jnp.float32)
    for g in range(kv_heads):
        mine = lax.div(row, per) == g
        key = jnp.where(mine, new_k[g : g + 1, :].astype(jnp.float32), key)
        value = jnp.where(mine, new_v[g : g + 1, :].astype(jnp.float32), value)
    own = jnp.sum(qv.astype(jnp.float32) * key, axis=1, keepdims=True) * scale
    top = jnp.maximum(jnp.max(scores, axis=1, keepdims=True), own)
    weights = jnp.where(valid, jnp.exp(scores - top), 0.0)
    own_weight = jnp.exp(own - top)
    total = jnp.sum(weights, axis=1, keepdims=True) + own_weight
    probs = pltpu.roll(weights / total, kv_heads, 1).astype(jnp.bfloat16)
    own_prob = (own_weight / total).astype(jnp.bfloat16).astype(jnp.float32)
    out[...] = (dot(probs, kvv) + own_prob * value).astype(out.dtype)


def layer_kernel(
    table, length, q, new_k, new_v, kv_hbm, tokens, gain, ids, gates, win_hbm, wout_hbm,
    attn_out, moe_out,
    kv, win, wout, xg, mg, grid_in, grid_out, acc, hid, pj, ybuf, r1, s2, r2, s3, r3, keep,
    local_sem, send_sem, gather_sem, r1_sem, r2_sem, r3_sem,
):
    z, x, c = lax.axis_index("expert"), lax.axis_index("attn"), lax.axis_index("tp")
    ranks = lax.axis_size("expert")
    rows, width = tokens.shape
    devices = ranks * 4
    total_rows = devices * rows
    kc = width // K_PARTS
    wj = width // J_PARTS
    units = wout.shape[0]
    slots = grid_in.shape[0]
    choices = ids.shape[0]

    def place_of(zz, xx, cc):
        return (cc * 2 + xx) * ranks + zz

    me = place_of(z, x, c)
    expert = (z * 2 + x) * 2 + c
    to_core, to_x = {"tp": 1 - c}, {"attn": 1 - x}
    z_next = [lax.rem(z + d, ranks) for d in range(1, ranks)]
    z_prev = [lax.rem(z + ranks - d, ranks) for d in range(1, ranks)]
    peers = [to_core, to_x] + [{"expert": zz} for zz in z_next]

    barrier = pltpu.get_barrier_semaphore()
    for peer in peers:
        pl.semaphore_signal(barrier, inc=1, device_id=peer, device_id_type=MESH)

    local = []

    def load(src, dst):
        copy = pltpu.make_async_copy(src, dst, local_sem.at[len(local)])
        copy.start()
        local.append(copy)

    load(kv_hbm, kv)
    in_tiles = win.shape[0] // UNIT_TILE
    for n in range(in_tiles):
        part = pl.ds(n * UNIT_TILE, UNIT_TILE)
        load(win_hbm.at[part], win.at[part])
    for n in range(units // UNIT_TILE):
        part = pl.ds(n * UNIT_TILE, UNIT_TILE)
        load(wout_hbm.at[part], wout.at[part])

    share = gates[...] / jnp.sum(gates[...], axis=0, keepdims=True)
    high = share.astype(jnp.bfloat16).astype(jnp.float32)
    low = share - high
    name = lax.broadcasted_iota(jnp.int32, (2 * LOW, rows), 0)
    meta = jnp.zeros((2 * LOW, rows), jnp.float32)
    chosen = ids[...]
    for k in range(choices):
        one = chosen[k : k + 1, :]
        meta = jnp.where(name == one, high[k : k + 1, :], meta)
        meta = jnp.where(name == one + LOW, low[k : k + 1, :], meta)
    same = lax.broadcasted_iota(jnp.int32, (rows, rows), 0) == lax.broadcasted_iota(
        jnp.int32, (rows, rows), 1
    )
    unit = jnp.where(same, 1.0, 0.0).astype(jnp.bfloat16)
    mg[me] = dot_nt(unit, meta.astype(jnp.bfloat16)).astype(jnp.bfloat16)
    floats = tokens[...].astype(jnp.float32)
    normed = floats * lax.rsqrt(jnp.mean(floats * floats, axis=1, keepdims=True) + epsilon)
    normed = (normed * gain[...]).astype(jnp.bfloat16)
    for k in range(K_PARTS):
        xg[k, me] = normed[:, k * kc : (k + 1) * kc]

    pl.semaphore_wait(barrier, len(peers))
    sent, across, used = [], [], [0]

    def push(src, dst, recv, peer):
        copy = pltpu.make_async_remote_copy(
            src_ref=src, dst_ref=dst, send_sem=send_sem.at[used[0]], recv_sem=recv,
            device_id=peer, device_id_type=MESH,
        )
        copy.start()
        used[0] += 1
        sent.append(copy)
        return copy

    def arrived(ref, recv):
        pltpu.make_async_remote_copy(
            src_ref=ref, dst_ref=ref, send_sem=send_sem.at[0], recv_sem=recv,
            device_id=to_core, device_id_type=MESH,
        ).wait_recv()

    def block(k, at):
        return mg.at[at] if k == 0 else xg.at[k - 1, at]

    def give(k, at, peer):
        push(block(k, at), block(k, at), gather_sem.at[k, at], peer)

    def take(k, at):
        arrived(block(k, at), gather_sem.at[k, at])

    def own_near(k):
        give(k, me, to_x)
        give(k, me, to_core)

    def own_far(k, i):
        give(k, me, {"expert": z_next[i]})

    def along_z(k):
        for i, zz in enumerate(z_prev):
            at = place_of(zz, x, c)
            take(k, at)
            if k and k < K_PARTS:
                own_far(k + 1, i)
            give(k, at, to_x)
            give(k, at, to_core)

    def along_x(k):
        for zz in [z] + z_prev:
            at = place_of(zz, 1 - x, c)
            take(k, at)
            give(k, at, to_core)

    def along_core(k):
        for xx in (x, 1 - x):
            for zz in [z] + z_prev:
                take(k, place_of(zz, xx, 1 - c))

    for k in range(2):
        for i in range(ranks - 1):
            own_far(k, i)
    for k in range(K_PARTS + 1):
        own_near(k)
    local[0].wait()
    attend_block(table, length, q, new_k, new_v, kv, attn_out)
    r_row = lax.broadcasted_iota(jnp.int32, (total_rows, total_rows), 0)
    r_col = lax.broadcasted_iota(jnp.int32, (total_rows, total_rows), 1)
    before = jnp.where(r_row > r_col, 1.0, 0.0).astype(jnp.bfloat16)
    after = jnp.where(r_row < r_col, 1.0, 0.0).astype(jnp.bfloat16)
    pj[...] = jnp.zeros_like(pj)
    along_z(0)
    along_z(1)
    along_x(0)
    along_core(0)

    routes = mg[...].reshape(total_rows, 2 * LOW)
    named = jnp.where(routes.astype(jnp.float32) > 0.0, 1.0, 0.0)
    lanes = lax.broadcasted_iota(jnp.int32, (total_rows, 2 * LOW), 1)
    named = jnp.where(lanes == expert, named, 0.0)
    named_b = named.astype(jnp.bfloat16)
    m_col = jnp.sum(named, axis=1, keepdims=True)
    at_col = jnp.sum(dot(before, named_b), axis=1, keepdims=True)
    ones = jnp.ones((16, 2 * LOW), jnp.bfloat16)
    m_row = dot_nt(ones, named_b)
    at_row = dot(m_row.astype(jnp.bfloat16), after)
    s_row = lax.broadcasted_iota(jnp.int32, (slots, total_rows), 0).astype(jnp.float32)
    grid_in[...] = jnp.where(
        (s_row == at_row[0:1, :]) & (m_row[0:1, :] > 0.5), 1.0, 0.0
    ).astype(jnp.bfloat16)
    s_col = lax.broadcasted_iota(jnp.int32, grid_out.shape, 1).astype(jnp.float32)
    grid_out[...] = jnp.where((s_col == at_col) & (m_col > 0.5), 1.0, 0.0).astype(jnp.bfloat16)
    picked = dot(grid_in[...], routes)
    p_lane = lax.broadcasted_iota(jnp.int32, (slots, 2 * LOW), 1)
    slot_share = jnp.sum(
        jnp.where((p_lane == expert) | (p_lane == expert + LOW), picked, 0.0), axis=1, keepdims=True
    )
    if K_PARTS > 1:
        along_z(2)
    along_x(1)

    for copy in local[1:]:
        copy.wait()
    for k in range(K_PARTS):
        if k + 2 < K_PARTS:
            along_z(k + 3)
        along_core(k + 1)
        rows_in = dot(grid_in[...], xg[k].reshape(total_rows, kc)).astype(jnp.bfloat16)

        def tile(n, _, k=k, rows_in=rows_in):
            start = pl.multiple_of(n * UNIT_TILE, UNIT_TILE)
            product = dot_nt(rows_in, win[pl.ds(start, UNIT_TILE), k * kc : (k + 1) * kc])
            acc[n] = product if k == 0 else acc[n] + product
            return 0

        lax.fori_loop(0, in_tiles, tile, 0)
        if k + 1 < K_PARTS:
            along_x(k + 2)

    for n in range(in_tiles // 2):
        gate = acc[n]
        hid[:, n * UNIT_TILE : (n + 1) * UNIT_TILE] = (
            gate / (1.0 + jnp.exp(-gate)) * acc[n + in_tiles // 2]
        ).astype(jnp.bfloat16)

    half = grid_out.shape[0] // 2

    def first(j):
        part = dot(hid[...], wout[:, j * wj : (j + 1) * wj]) * slot_share
        pj[0:slots, :] = part.astype(jnp.bfloat16)
        for cc in (1 - c, c):
            spread = dot(grid_out[pl.ds(pl.multiple_of(cc * half, half), half), :], pj[...])
            ybuf[j, cc] = spread.astype(jnp.bfloat16).reshape(2, half // 2, wj)
            if cc is not c:
                push(ybuf.at[j, cc], r1.at[j], r1_sem.at[j], to_core)

    def second(j):
        arrived(r1.at[j], r1_sem.at[j])
        s2[j] = (
            ybuf[j, c, 1 - x].astype(jnp.float32) + r1[j, 1 - x].astype(jnp.float32)
        ).astype(jnp.bfloat16)
        if j:
            across[j - 1].wait_send()
        across.append(push(s2.at[j], r2.at[j], r2_sem.at[j], to_x))

    def third(j):
        arrived(r2.at[j], r2_sem.at[j])
        for zz in z_next + [z]:
            part = pl.ds(pl.multiple_of(zz * rows, rows), rows)
            value = (
                ybuf[j, c, x, part, :].astype(jnp.float32)
                + r1[j, x, part, :].astype(jnp.float32)
                + r2[j, part, :].astype(jnp.float32)
            )
            if zz is z:
                keep[j] = value
            else:
                s3[j, zz] = value.astype(jnp.bfloat16)
                push(s3.at[j, zz], r3.at[j, z], r3_sem.at[j, z], {"expert": zz})

    def fourth(j):
        value = keep[j]
        for zz in z_prev:
            arrived(r3.at[j, zz], r3_sem.at[j, zz])
            value = value + r3[j, zz].astype(jnp.float32)
        moe_out[:, j * wj : (j + 1) * wj] = value.astype(moe_out.dtype)

    for step in range(J_PARTS + 4):
        for lag, stage in ((0, first), (1, second), (2, third), (4, fourth)):
            if 0 <= step - lag < J_PARTS:
                stage(step - lag)
    for copy in sent:
        if not any(copy is early for early in across[:-1]):
            copy.wait_send()


def fused_layer(
    queries, new_keys, new_values, kv_cache, block_tables, cache_lengths,
    tokens, gain, expert_ids, gate_weights, w_in, w_out,
):
    rows, width = tokens.shape
    ranks = lax.axis_size("expert")
    devices = 4 * ranks
    experts = devices
    most = max(2, rows * TOP // experts + 1)
    slots = -(-most * devices // 16) * 16
    padded = -(-slots // 128) * 128
    units = w_out.shape[1]
    total = devices * rows
    kc, wj = width // K_PARTS, width // J_PARTS
    heads, size = queries.shape[1:]
    bf, f32 = jnp.bfloat16, jnp.float32
    kv = kv_cache.reshape(-1, size)
    sends = 15 * (K_PARTS + 1) + (2 + ranks - 1) * J_PARTS
    vmem = pl.BlockSpec(memory_space=pltpu.VMEM)
    smem = pl.BlockSpec(memory_space=pltpu.SMEM)
    anyw = pl.BlockSpec(memory_space=pl.ANY)
    attn_out, moe_out = pl.pallas_call(
        layer_kernel,
        out_shape=(
            jax.ShapeDtypeStruct((heads, size), bf),
            jax.ShapeDtypeStruct((rows, width), bf),
        ),
        in_specs=[smem, smem, vmem, vmem, vmem, anyw, vmem, vmem, vmem, vmem, anyw, anyw],
        out_specs=(vmem, vmem),
        scratch_shapes=[
            pltpu.VMEM(kv.shape, bf),
            pltpu.VMEM((2 * units, width), bf),
            pltpu.VMEM((units, width), bf),
            pltpu.VMEM((K_PARTS, devices, rows, kc), bf),
            pltpu.VMEM((devices, rows, 2 * LOW), bf),
            pltpu.VMEM((slots, total), bf),
            pltpu.VMEM((total, padded), bf),
            pltpu.VMEM((2 * units // UNIT_TILE, slots, UNIT_TILE), f32),
            pltpu.VMEM((slots, units), bf),
            pltpu.VMEM((padded, wj), bf),
            pltpu.VMEM((J_PARTS, 2, 2, total // 4, wj), bf),
            pltpu.VMEM((J_PARTS, 2, total // 4, wj), bf),
            pltpu.VMEM((J_PARTS, total // 4, wj), bf),
            pltpu.VMEM((J_PARTS, total // 4, wj), bf),
            pltpu.VMEM((J_PARTS, ranks, rows, wj), bf),
            pltpu.VMEM((J_PARTS, ranks, rows, wj), bf),
            pltpu.VMEM((J_PARTS, rows, wj), f32),
            pltpu.SemaphoreType.DMA((1 + 3 * units // UNIT_TILE,)),
            pltpu.SemaphoreType.DMA((sends,)),
            pltpu.SemaphoreType.DMA((K_PARTS + 1, devices)),
            pltpu.SemaphoreType.DMA((J_PARTS,)),
            pltpu.SemaphoreType.DMA((J_PARTS,)),
            pltpu.SemaphoreType.DMA((J_PARTS, ranks)),
        ],
        compiler_params=pltpu.CompilerParams(
            collective_id=0, has_side_effects=True, vmem_limit_bytes=56 * 1024 * 1024
        ),
    )(
        block_tables, cache_lengths, queries[0], new_keys[0], new_values[0], kv,
        tokens, gain.reshape(1, width), expert_ids.T, gate_weights.T,
        w_in.reshape(2 * units, width), w_out.reshape(units, width),
    )
    return (attn_out.reshape(1, heads, size), moe_out)


def attend(queries, new_keys, new_values, kv_cache, block_tables, cache_lengths):
    rows, heads, size = queries.shape
    kv_heads = new_keys.shape[1]
    grouped = queries.reshape(rows, kv_heads, heads // kv_heads, size)
    pages = kv_cache[block_tables]
    span = pages.shape[1] * pages.shape[2]
    pages = pages.reshape(rows, span, 2, kv_heads, size)
    scale = size ** (-0.5)
    scores = (
        jnp.einsum("rkgd,rlkd->rkgl", grouped, pages[:, :, 0], preferred_element_type=jnp.float32)
        * scale
    )
    inside = jnp.arange(span, dtype=jnp.int32)[None, :] < cache_lengths[:, None]
    scores = jnp.where(inside[:, None, None, :], scores, -jnp.inf)
    own = jnp.einsum("rkgd,rkd->rkg", grouped, new_keys, preferred_element_type=jnp.float32) * scale
    top = jnp.maximum(jnp.max(scores, axis=3), own)
    weights = jnp.exp(scores - top[..., None])
    own_weight = jnp.exp(own - top)
    total = jnp.sum(weights, axis=3) + own_weight
    probs = (weights / total[..., None]).astype(jnp.bfloat16)
    own_prob = (own_weight / total).astype(jnp.bfloat16)
    mixed = jnp.einsum("rkgl,rlkd->rkgd", probs, pages[:, :, 1], preferred_element_type=jnp.float32)
    mixed = (
        mixed
        + own_prob.astype(jnp.float32)[..., None] * new_values.astype(jnp.float32)[:, :, None, :]
    )
    return mixed.astype(jnp.bfloat16).reshape(rows, heads, size)


def expert_part(rows_in, weights_in, weights_out):
    both = jnp.einsum("nd,gud->gnu", rows_in, weights_in, preferred_element_type=jnp.float32)
    hidden = (jax.nn.silu(both[0]) * both[1]).astype(jnp.bfloat16)
    return jnp.dot(hidden, weights_out, preferred_element_type=jnp.float32).astype(jnp.bfloat16)


def per_device(
    queries,
    new_keys,
    new_values,
    kv_cache,
    block_tables,
    cache_lengths,
    tokens,
    gain,
    expert_ids,
    gate_weights,
    w_in,
    w_out,
):
    ranks, cores = lax.axis_size("expert"), lax.axis_size("tp")
    fits = ranks * 4 * tokens.shape[0] <= 512 and queries.shape[0] == 1
    if lax.axis_size("attn") == 2 and cores == 2 and fits:
        return fused_layer(
            queries, new_keys, new_values, kv_cache, block_tables, cache_lengths,
            tokens, gain, expert_ids, gate_weights, w_in, w_out,
        )
    attn_out = attend(queries, new_keys, new_values, kv_cache, block_tables, cache_lengths)
    rows, width = tokens.shape
    ranks = lax.axis_size("expert")
    peers = lax.axis_size(("attn", "tp"))
    slices = peers // EXP_RANK
    experts = EXP_RANK * ranks
    most = max(2, rows * TOP // experts + 1)
    floats = tokens.astype(jnp.float32)
    normed = (
        floats * lax.rsqrt(jnp.mean(floats * floats, axis=1, keepdims=True) + epsilon) * gain
    ).astype(jnp.bfloat16)
    chosen = expert_ids.reshape(-1)
    onehot = (chosen[:, None] == jnp.arange(experts, dtype=jnp.int32)[None, :]).astype(jnp.int32)
    earlier = jnp.cumsum(onehot, axis=0) - onehot
    targets = chosen * most + jnp.sum(earlier * onehot, axis=1)
    picks = (jnp.arange(experts * most, dtype=jnp.int32)[:, None] == targets[None, :]).astype(
        jnp.int32
    )
    picks = jnp.sum(picks.reshape(experts * most, rows, TOP), axis=2).astype(jnp.bfloat16)
    buckets = jnp.dot(picks, normed, preferred_element_type=jnp.float32).astype(jnp.bfloat16)
    buckets = buckets.reshape(experts, most, width)
    grouped = buckets.reshape(ranks, EXP_RANK, most, width)
    copies = jnp.repeat(grouped, slices, axis=1)
    in_rank = lax.all_to_all(copies, ("attn", "tp"), split_axis=1, concat_axis=1, tiled=True)
    arrived = lax.all_to_all(in_rank, "expert", split_axis=0, concat_axis=0, tiled=True)
    partial_rows = expert_part(arrived.reshape(-1, width), w_in[0], w_out[0])
    partial_rows = partial_rows.reshape(ranks, peers, most, width)
    returned = lax.all_to_all(partial_rows, "expert", split_axis=0, concat_axis=0, tiled=True)
    gathered = lax.all_to_all(returned, ("attn", "tp"), split_axis=1, concat_axis=1, tiled=True)
    summed = jnp.sum(
        gathered.reshape(ranks, EXP_RANK, slices, most, width).astype(jnp.float32), axis=2
    )
    home = summed.astype(jnp.bfloat16).reshape(experts, most, width)
    flat_home = home.reshape(experts * most, width)
    shares = gate_weights / jnp.sum(gate_weights, axis=1, keepdims=True)
    placed = targets.reshape(rows, TOP)
    mixed = jnp.zeros((rows, width), jnp.float32)
    for column in range(TOP):
        mixed = mixed + shares[:, column : column + 1] * flat_home[placed[:, column]].astype(
            jnp.float32
        )
    return (attn_out, mixed.astype(jnp.bfloat16))


def solution(mesh):
    return jax.shard_map(
        per_device,
        mesh=mesh,
        in_specs=(
            P(("groups", "expert", "attn"), "tp", None),
            P(("groups", "expert", "attn"), "tp", None),
            P(("groups", "expert", "attn"), "tp", None),
            P(("groups", "expert", "attn"), None, None, "tp", None),
            P(("groups", "expert", "attn"), None),
            P(("groups", "expert", "attn")),
            P(("groups", "expert", "attn", "tp"), None),
            P(),
            P(("groups", "expert", "attn", "tp"), None),
            P(("groups", "expert", "attn", "tp"), None),
            P(("expert", "attn", "tp"), None, None, None),
            P(("expert", "attn", "tp"), None, None),
        ),
        out_specs=(
            P(("groups", "expert", "attn"), "tp", None),
            P(("groups", "expert", "attn", "tp"), None),
        ),
        check_vma=False,
    )
```
